32 devices in a mesh: state: 4 (over y, core), aux: 2 (over x), cond: 4 (over z).
Axes of the slice: x: 2, y: 2, z: 4, core: 2. Of those that a mesh axis runs over, the one named last changes fastest.
Arguments:
- cond_pairs: float32 [8, 1024, 1024], P('aux', 'cond', 'state'), may hold values from -0.1875 to 0.1875
- val_pairs: float32 [8, 512, 512], P('aux', 'state', 'cond'), may hold values from -0.25 to 0.25
- screened: float32 [8, 8], replicated, may hold values from -0.75 to 0.75
- trials: float32 [8, 1024, 512], P('state', 'cond'), may hold values from -6 to 6
Outputs:
- response: float32 [8, 1024, 512], P('state', 'cond')
The draws below stay inside these ranges and needn't reach their ends.
All inputs are finite; a program needn't handle non-finite values.
Results may differ from the reference program's by a relative error of at most 0.0001.
Values sent between devices are 32-bit elements; how exact they have to be, the bound alone decides.
A program may use at most 64 MiB of HBM per device.

```python
import jax
import jax.numpy as jnp
from jax import lax

NC = 1024
NV = 512
NT = 8
NAUX = 8


def block_scale(rng, extent, pieces, least, top_value):
    gain = 1.0
    for dim, shards_of in pieces:
        draws = jax.random.uniform(jax.random.fold_in(jax.random.fold_in(rng, 6), dim), (shards_of,), jnp.float32, least / len(pieces), top_value / len(pieces))
        gain = gain * jnp.repeat(jnp.exp(draws), extent[dim] // shards_of).reshape((-1,) + (1,) * (len(extent) - 1 - dim))
    return gain


def gaussian(key, shape, deviation, reach, shards=(), dtype=jnp.bfloat16):
    values = jax.random.normal(key, shape, jnp.float32) * deviation
    if len(shards) > 0:
        values = block_scale(key, shape, shards, -0.22, 0.18) * values
    return jnp.clip(values, min=-reach, max=reach).astype(dtype)


def setup_inputs(seed: int = 0) -> dict:
    keys = jax.random.split(jax.random.key(seed), 5)
    return {
        "cond_pairs": gaussian(keys[0], (NAUX, NC, NC), NC ** -0.5, 0.1875, ((0, 2), (1, 4), (2, 4)), jnp.float32),
        "val_pairs": gaussian(keys[1], (NAUX, NV, NV), NV ** -0.5, 0.25, ((0, 2), (1, 4), (2, 4)), jnp.float32),
        "screened": gaussian(keys[2], (NAUX, NAUX), (NAUX * NAUX) ** -0.5, 0.75, (), jnp.float32),
        "trials": gaussian(keys[3], (NT, NC, NV), 1.0, 6.0, ((0, 4), (1, 4)), jnp.float32),
    }


highest = lax.Precision.HIGHEST


def reference(cond_pairs, val_pairs, screened, trials):
    coupled = jnp.einsum("pq,qab->pab", screened, val_pairs, precision=highest)

    def add_aux(running, scanned):
        slab_block, pair_block = scanned
        mixture = jnp.einsum("cd,ndv->ncv", slab_block, trials, precision=highest)
        return running + jnp.einsum("ncv,vw->ncw", mixture, pair_block, precision=highest), None

    start_value = jnp.zeros(trials.shape, jnp.float32)
    response, unused = lax.scan(add_aux, start_value, (cond_pairs, coupled))
    return response
```

```python
import functools

import jax
import jax.numpy as jnp
from jax import lax
from jax.experimental import pallas as pl
from jax.experimental.pallas import tpu as pltpu
from jax.sharding import PartitionSpec as P

highest = lax.Precision.HIGHEST
MESH = pl.DeviceIdType.MESH
UP, DOWN = 0, 1


def split(value):
    high = value.astype(jnp.bfloat16)
    low = (value - high.astype(jnp.float32)).astype(jnp.bfloat16)
    return high, low


def dot3(a_high, a_low, b_high, b_low):
    dot = functools.partial(jnp.dot, preferred_element_type=jnp.float32)
    return dot(a_high, b_high) + dot(a_high, b_low) + dot(a_low, b_high)


def kernel(
    n_cond,
    screened,
    b_own,
    v_own,
    x_own,
    out,
    v_got,
    b_raw,
    b_high,
    b_low,
    x_raw,
    c_raw,
    c_high,
    c_low,
    mixed,
    y_part,
    y_got,
    v_sems,
    b_sems,
    xz_sems,
    xx_sems,
    cz_sems,
    cy_sems,
    ck_sems,
    cf_sems,
    y_sems,
):
    s = lax.axis_index("state")
    a = lax.axis_index("aux")
    z = lax.axis_index("cond")
    aux_dev, rows, depth = b_own.shape
    n_trials = x_own.shape[0]
    half = rows // 2
    blk_v, blk_w = v_own.shape[1], v_own.shape[2]
    core_s = s + 1 - 2 * lax.rem(s, 2)
    y_s = lax.rem(s + 2, 4)
    far_s = lax.rem(core_s + 2, 4)
    x_mate = {"aux": 1 - a}
    y_mate = {"state": y_s}
    core_mate = {"state": core_s}
    z_next = ({"cond": z + 1}, {"cond": z - 1})
    has_next = (z + 1 < n_cond, z > 0)

    barrier = pltpu.get_barrier_semaphore()
    for mate in (x_mate, y_mate, core_mate):
        pl.semaphore_signal(barrier, inc=1, device_id=mate, device_id_type=MESH)
    for way in (UP, DOWN):

        @pl.when(has_next[way])
        def _():
            pl.semaphore_signal(barrier, inc=1, device_id=z_next[way], device_id_type=MESH)

    pl.semaphore_wait(
        barrier, 3 + has_next[UP].astype(jnp.int32) + has_next[DOWN].astype(jnp.int32)
    )

    sent = []

    def copy(src, dst, sems, index, mate):
        return pltpu.make_async_remote_copy(
            src_ref=src,
            dst_ref=dst,
            send_sem=sems.at[(0, *index)],
            recv_sem=sems.at[(1, *index)],
            device_id=mate,
            device_id_type=MESH,
        )

    def send(src, dst, sems, index, mate, where=None):
        if where is None:
            copy(src, dst, sems, index, mate).start()
        else:

            @pl.when(where)
            def _():
                copy(src, dst, sems, index, mate).start()

        sent.append((src, dst, sems, index, mate, where))

    def wait(dst, sems, index, mate):
        copy(dst, dst, sems, index, mate).wait_recv()

    def arrives(way, step):
        return z - step >= 0 if way == UP else z + step < n_cond

    def origin(way, step):
        return z - step if way == UP else z + step

    def x_slot(n, block, side):
        return x_raw.at[n, block, pl.ds(side * half, half)]

    def send_x_own(n):
        for way in (UP, DOWN):
            send(
                x_own.at[n, pl.ds(a * half, half)],
                x_slot(n, z, a),
                xz_sems,
                (n, way, 1),
                z_next[way],
                has_next[way],
            )

    def pass_x(n, step):
        for way in (UP, DOWN):
            here = arrives(way, step)
            slot = x_slot(n, jnp.clip(origin(way, step), 0, n_cond - 1), a)

            @pl.when(here)
            def _():
                wait(slot, xz_sems, (n, way, step), z_next[way])

            if step + 1 < n_cond:
                send(
                    slot, slot, xz_sems, (n, way, step + 1), z_next[way],
                    jnp.logical_and(here, has_next[way]),
                )
            send(slot, slot, xx_sems, (n, way, step), x_mate, here)

    def c_slot(state, block):
        return c_raw.at[state, block]

    def pass_c(step):
        for way in (UP, DOWN):
            here = arrives(way, step)
            slot = c_slot(s, jnp.clip(origin(way, step), 0, n_cond - 1))

            @pl.when(here)
            def _():
                wait(slot, cz_sems, (way, step), z_next[way])

            if step + 1 < n_cond:
                send(
                    slot, slot, cz_sems, (way, step + 1), z_next[way],
                    jnp.logical_and(here, has_next[way]),
                )
            send(slot, slot, cy_sems, (way, step), y_mate, here)
            send(slot, slot, ck_sems, (way, step), core_mate, here)

    def split_b(state, source):
        for p in range(aux_dev):
            high, low = split(source[p])
            b_high[state, p] = high
            b_low[state, p] = low

    def mix(n, block, value, first=False):
        x_high, x_low = split(value)

        @pl.loop(0, aux_dev)
        def _(p):
            term = dot3(b_high[block, p], b_low[block, p], x_high, x_low)
            if first:
                mixed[n, p] = term
            else:
                mixed[n, p] += term

    def mix_step(n, step):
        for way in (UP, DOWN):
            here = arrives(way, step)
            block = jnp.clip(origin(way, step), 0, n_cond - 1)

            @pl.when(here)
            def _():
                wait(x_slot(n, block, 1 - a), xx_sems, (n, way, step), x_mate)
                mix(n, block, x_raw[n, block])

    def apply(n, first, size):
        def term(p):
            m_high, m_low = split(mixed[n, p, first : first + size])
            return dot3(m_high, m_low, c_high[p], c_low[p])

        y_part[n, first : first + size] = term(0)

        @pl.loop(1, aux_dev)
        def _(p):
            y_part[n, first : first + size] += term(p)

        send(
            y_part.at[n, pl.ds(first, size)],
            y_got.at[n, pl.ds(first, size)],
            y_sems,
            (n, first // half),
            x_mate,
        )

    send(v_own, v_got, v_sems, (0,), x_mate)
    send_x_own(0)
    send(b_own, b_raw.at[s], b_sems, (0,), y_mate)
    send(b_own, b_raw.at[s], b_sems, (1,), core_mate)
    split_b(s, b_own)

    wait(v_got, v_sems, (0,), x_mate)
    for p in range(aux_dev):
        row = a * aux_dev + p
        total = screened[row, a * aux_dev] * v_own[0]
        for q in range(1, aux_dev):
            total += screened[row, a * aux_dev + q] * v_own[q]
        for q in range(aux_dev):
            total += screened[row, (1 - a) * aux_dev + q] * v_got[q]
        c_raw[s, z, p] = total
    own = c_slot(s, z)
    for way in (UP, DOWN):
        send(own, own, cz_sems, (way, 1), z_next[way], has_next[way])
    send(own, own, cy_sems, (UP, 0), y_mate)
    send(own, own, ck_sems, (UP, 0), core_mate)

    for step in range(1, n_cond):
        pass_x(0, step)
        if step == 1:
            pass_c(1)
    for n in range(1, n_trials):
        send_x_own(n)
    wait(b_raw.at[core_s], b_sems, (1,), core_mate)
    split_b(core_s, b_raw.at[core_s])
    wait(b_raw.at[y_s], b_sems, (0,), y_mate)
    send(b_raw.at[y_s], b_raw.at[y_s], b_sems, (2,), core_mate)
    for step in range(2, n_cond):
        pass_c(step)
    split_b(y_s, b_raw.at[y_s])
    wait(b_raw.at[far_s], b_sems, (2,), core_mate)
    split_b(far_s, b_raw.at[far_s])
    mix(0, z, x_own[0], first=True)
    for n in range(1, n_trials):
        pass_x(n, 1)
    for step in range(1, n_cond):
        mix_step(0, step)

    def each_c(sems, action):
        action((UP, 0), z, None)
        for step in range(1, n_cond):
            for way in (UP, DOWN):
                block = jnp.clip(origin(way, step), 0, n_cond - 1)
                action((way, step), block, arrives(way, step))

    def under(where, run):
        if where is None:
            run()
        else:
            pl.when(where)(run)

    def from_y(index, block, where):
        slot = c_slot(y_s, block)
        under(where, lambda: wait(slot, cy_sems, index, y_mate))
        send(slot, slot, cf_sems, index, core_mate, where)

    each_c(cy_sems, from_y)
    for n in range(1, n_trials):
        for step in range(2, n_cond):
            pass_x(n, step)

    def from_core(index, block, where):
        under(where, lambda: wait(c_slot(core_s, block), ck_sems, index, core_mate))

    def from_far(index, block, where):
        under(where, lambda: wait(c_slot(far_s, block), cf_sems, index, core_mate))

    each_c(ck_sems, from_core)
    each_c(cf_sems, from_far)
    for state in range(c_raw.shape[0]):
        for block in range(n_cond):
            place = (
                slice(None),
                slice(state * blk_v, (state + 1) * blk_v),
                slice(block * blk_w, (block + 1) * blk_w),
            )
            high, low = split(c_raw[state, block])
            c_high[place] = high
            c_low[place] = low

    apply(0, 0, half)
    apply(0, half, half)
    for n in range(1, n_trials):
        mix(n, z, x_own[n], first=True)
        for step in range(1, n_cond):
            mix_step(n, step)
        apply(n, 0, half)
        apply(n, half, half)
    for n in range(n_trials):
        for part in range(2):
            place = pl.ds(part * half, half)
            wait(y_got.at[n, place], y_sems, (n, part), x_mate)
            out[n, part * half : (part + 1) * half] = (
                y_part[n, part * half : (part + 1) * half]
                + y_got[n, part * half : (part + 1) * half]
            )
    for src, dst, sems, index, mate, where in sent:
        under(where, lambda: copy(src, dst, sems, index, mate).wait_send())


def fused(n_state, n_cond, cond_pairs, val_pairs, screened, trials):
    aux_dev, rows, depth = cond_pairs.shape
    n_trials, _, width = trials.shape
    blk_v, blk_w = val_pairs.shape[1:]
    f32, bf16 = jnp.float32, jnp.bfloat16
    dma = pltpu.SemaphoreType.DMA
    vmem = pl.BlockSpec(memory_space=pltpu.VMEM)
    macs = aux_dev * n_trials * rows * width * (n_state * depth + width)
    return pl.pallas_call(
        functools.partial(kernel, n_cond),
        out_shape=jax.ShapeDtypeStruct(trials.shape, f32),
        in_specs=[pl.BlockSpec(memory_space=pltpu.SMEM), vmem, vmem, vmem],
        out_specs=vmem,
        scratch_shapes=[
            pltpu.VMEM(val_pairs.shape, f32),
            pltpu.VMEM((n_state, *cond_pairs.shape), f32),
            pltpu.VMEM((n_state, *cond_pairs.shape), bf16),
            pltpu.VMEM((n_state, *cond_pairs.shape), bf16),
            pltpu.VMEM((n_trials, n_cond, rows, width), f32),
            pltpu.VMEM((n_state, n_cond, *val_pairs.shape), f32),
            pltpu.VMEM((aux_dev, width, width), bf16),
            pltpu.VMEM((aux_dev, width, width), bf16),
            pltpu.VMEM((n_trials, aux_dev, rows, width), f32),
            pltpu.VMEM(trials.shape, f32),
            pltpu.VMEM(trials.shape, f32),
            dma((2, 1)),
            dma((2, 3)),
            dma((2, n_trials, 2, n_cond)),
            dma((2, n_trials, 2, n_cond)),
            dma((2, 2, n_cond)),
            dma((2, 2, n_cond)),
            dma((2, 2, n_cond)),
            dma((2, 2, n_cond)),
            dma((2, n_trials, 2)),
        ],
        compiler_params=pltpu.CompilerParams(
            collective_id=0, has_side_effects=True, vmem_limit_bytes=56 * 1024 * 1024
        ),
        cost_estimate=pl.CostEstimate(
            flops=6 * macs, bytes_accessed=4 * (2 * trials.size + cond_pairs.size), transcendentals=0
        ),
    )(screened, cond_pairs, val_pairs, trials)


def gathered(cond_pairs, val_pairs, screened, trials):
    aux_dev = cond_pairs.shape[0]
    aux_first = lax.axis_index("aux") * aux_dev
    own_rows = lax.dynamic_slice_in_dim(screened, aux_first, aux_dev, 0)
    coupled = jnp.einsum(
        "pq,qab->pab",
        own_rows,
        lax.all_gather(val_pairs, "aux", axis=0, tiled=True),
        precision=highest,
    )
    n_state = lax.axis_size("state")
    n_cond = lax.axis_size("cond")
    rows_state = coupled.shape[1]
    cols_cond = coupled.shape[2]
    pieces = lax.all_gather(coupled[None], ("state", "cond"), axis=0, tiled=True)
    coupled_full = pieces.reshape(n_state, n_cond, aux_dev, rows_state, cols_cond)
    coupled_full = coupled_full.transpose(2, 0, 3, 1, 4).reshape(
        aux_dev, n_state * rows_state, n_cond * cols_cond
    )
    everything = lax.all_gather(trials, "cond", axis=1, tiled=True)
    mixture = jnp.einsum(
        "pcd,ndv->pncv",
        lax.all_gather(cond_pairs, "state", axis=2, tiled=True),
        everything,
        precision=highest,
    )
    partial_value = jnp.einsum("pncv,pvw->ncw", mixture, coupled_full, precision=highest)
    return lax.psum(partial_value, "aux")


def solution(mesh):
    n_state, n_cond = mesh.shape["state"], mesh.shape["cond"]
    in_specs = (P("aux", "cond", "state"), P("aux", "state", "cond"), P(), P("state", "cond", None))
    out_specs = P("state", "cond", None)
    if mesh.shape["aux"] == 2 and n_state == 4 and n_cond == n_state:
        per_device = functools.partial(fused, n_state, n_cond)
    else:
        per_device = gathered
    return jax.shard_map(
        per_device, mesh=mesh, in_specs=in_specs, out_specs=out_specs, check_vma=False
    )
```

```python
import functools

import jax
import jax.numpy as jnp
from jax import lax
from jax.experimental import pallas as pl
from jax.experimental.pallas import tpu as pltpu
from jax.sharding import PartitionSpec as P

highest = lax.Precision.HIGHEST
MESH = pl.DeviceIdType.MESH
UP, DOWN = 0, 1


def split(value):
    high = value.astype(jnp.bfloat16)
    low = (value - high.astype(jnp.float32)).astype(jnp.bfloat16)
    return high, low


def dot3(a_high, a_low, b_high, b_low):
    dot = functools.partial(jnp.dot, preferred_element_type=jnp.float32)
    return dot(a_high, b_high) + dot(a_high, b_low) + dot(a_low, b_high)


def kernel(
    n_cond,
    screened,
    b_own,
    v_own,
    x_own,
    out,
    v_got,
    b_raw,
    b_high,
    b_low,
    x_raw,
    c_raw,
    mixed,
    m_high,
    m_low,
    y_part,
    y_got,
    v_sems,
    b_sems,
    xz_sems,
    xx_sems,
    cz_sems,
    cy_sems,
    ck_sems,
    cf_sems,
    y_sems,
):
    s = lax.axis_index("state")
    a = lax.axis_index("aux")
    z = lax.axis_index("cond")
    aux_dev, rows, depth = b_own.shape
    n_trials = x_own.shape[0]
    half = rows // 2
    blk_v, blk_w = v_own.shape[1], v_own.shape[2]
    core_s = s + 1 - 2 * lax.rem(s, 2)
    y_s = lax.rem(s + 2, 4)
    far_s = lax.rem(core_s + 2, 4)
    x_mate = {"aux": 1 - a}
    y_mate = {"state": y_s}
    core_mate = {"state": core_s}
    z_next = ({"cond": z + 1}, {"cond": z - 1})
    has_next = (z + 1 < n_cond, z > 0)

    barrier = pltpu.get_barrier_semaphore()
    for mate in (x_mate, y_mate, core_mate):
        pl.semaphore_signal(barrier, inc=1, device_id=mate, device_id_type=MESH)
    for way in (UP, DOWN):

        @pl.when(has_next[way])
        def _():
            pl.semaphore_signal(barrier, inc=1, device_id=z_next[way], device_id_type=MESH)

    pl.semaphore_wait(
        barrier, 3 + has_next[UP].astype(jnp.int32) + has_next[DOWN].astype(jnp.int32)
    )

    sent = []

    def copy(src, dst, sems, index, mate):
        return pltpu.make_async_remote_copy(
            src_ref=src,
            dst_ref=dst,
            send_sem=sems.at[(0, *index)],
            recv_sem=sems.at[(1, *index)],
            device_id=mate,
            device_id_type=MESH,
        )

    def send(src, dst, sems, index, mate, where=None):
        if where is None:
            copy(src, dst, sems, index, mate).start()
        else:

            @pl.when(where)
            def _():
                copy(src, dst, sems, index, mate).start()

        sent.append((src, dst, sems, index, mate, where))

    def wait(dst, sems, index, mate):
        copy(dst, dst, sems, index, mate).wait_recv()

    def arrives(way, step):
        return z - step >= 0 if way == UP else z + step < n_cond

    def origin(way, step):
        return z - step if way == UP else z + step

    def x_slot(n, block, side):
        return x_raw.at[n, block, pl.ds(side * half, half)]

    def send_x_own(n):
        for way in (UP, DOWN):
            send(
                x_own.at[n, pl.ds(a * half, half)],
                x_slot(n, z, a),
                xz_sems,
                (n, way, 1),
                z_next[way],
                has_next[way],
            )

    def pass_x(n, step):
        for way in (UP, DOWN):
            here = arrives(way, step)
            slot = x_slot(n, jnp.clip(origin(way, step), 0, n_cond - 1), a)

            @pl.when(here)
            def _():
                wait(slot, xz_sems, (n, way, step), z_next[way])

            if step + 1 < n_cond:
                send(
                    slot, slot, xz_sems, (n, way, step + 1), z_next[way],
                    jnp.logical_and(here, has_next[way]),
                )
            send(slot, slot, xx_sems, (n, way, step), x_mate, here)

    def c_slot(state, block):
        return c_raw.at[state, block]

    def pass_c(step):
        for way in (UP, DOWN):
            here = arrives(way, step)
            slot = c_slot(s, jnp.clip(origin(way, step), 0, n_cond - 1))

            @pl.when(here)
            def _():
                wait(slot, cz_sems, (way, step), z_next[way])

            if step + 1 < n_cond:
                send(
                    slot, slot, cz_sems, (way, step + 1), z_next[way],
                    jnp.logical_and(here, has_next[way]),
                )
            send(slot, slot, cy_sems, (way, step), y_mate, here)
            send(slot, slot, ck_sems, (way, step), core_mate, here)

    def split_b(state, source):
        for p in range(aux_dev):
            high, low = split(source[p])
            b_high[state, p] = high
            b_low[state, p] = low

    def mix(n, block, value, first=False):
        x_high, x_low = split(value)

        @pl.loop(0, aux_dev)
        def _(p):
            term = dot3(b_high[block, p], b_low[block, p], x_high, x_low)
            if first:
                mixed[n, p] = term
            else:
                mixed[n, p] += term

    def mix_step(step):
        for way in (UP, DOWN):
            here = arrives(way, step)
            block = jnp.clip(origin(way, step), 0, n_cond - 1)

            @pl.when(here)
            def _():
                for n in range(n_trials):
                    wait(x_slot(n, block, 1 - a), xx_sems, (n, way, step), x_mate)
                    mix(n, block, x_raw[n, block])

    def from_y(index, block):
        slot = c_slot(y_s, block)
        wait(slot, cy_sems, index, y_mate)
        copy(slot, slot, cf_sems, index, core_mate).start()

    def apply(index, block):
        wait(c_slot(core_s, block), ck_sems, index, core_mate)
        wait(c_slot(far_s, block), cf_sems, index, core_mate)

        @pl.loop(0, aux_dev)
        def _(p):
            c_high, c_low = split(c_raw[:, block, p].reshape(-1, blk_w))
            for n in range(n_trials):
                term = dot3(m_high[n, p], m_low[n, p], c_high, c_low)
                prior = y_part[block, n]
                y_part[block, n] = jnp.where(p == 0, term, prior + term)

        copy(y_part.at[block], y_got.at[block], y_sems, index, x_mate).start()

    def finish(index, block):
        wait(y_got.at[block], y_sems, index, x_mate)
        columns = pl.ds(pl.multiple_of(block * blk_w, blk_w), blk_w)
        for n in range(n_trials):
            out[n, :, columns] = y_part[block, n] + y_got[block, n]

    def at_step(step, *actions):
        for way in (UP, DOWN):
            block = jnp.clip(origin(way, step), 0, n_cond - 1)

            @pl.when(arrives(way, step))
            def _():
                for action in actions:
                    action((way, step), block)

    send(v_own, v_got, v_sems, (0,), x_mate)
    for n in range(n_trials):
        send_x_own(n)
    send(b_own, b_raw.at[s], b_sems, (0,), y_mate)
    send(b_own, b_raw.at[s], b_sems, (1,), core_mate)
    split_b(s, b_own)

    wait(v_got, v_sems, (0,), x_mate)
    for p in range(aux_dev):
        row = a * aux_dev + p
        total = screened[row, a * aux_dev] * v_own[0]
        for q in range(1, aux_dev):
            total += screened[row, a * aux_dev + q] * v_own[q]
        for q in range(aux_dev):
            total += screened[row, (1 - a) * aux_dev + q] * v_got[q]
        c_raw[s, z, p] = total
    own = c_slot(s, z)
    own_index = (UP, 0)
    send(own, own, cy_sems, own_index, y_mate)
    send(own, own, ck_sems, own_index, core_mate)

    def pass_all(step):
        for n in range(n_trials):
            pass_x(n, step)

    for step in range(1, n_cond - 1):
        pass_all(step)
    for way in (UP, DOWN):
        send(own, own, cz_sems, (way, 1), z_next[way], has_next[way])
    wait(b_raw.at[y_s], b_sems, (0,), y_mate)
    send(b_raw.at[y_s], b_raw.at[y_s], b_sems, (2,), core_mate)
    wait(b_raw.at[core_s], b_sems, (1,), core_mate)
    split_b(core_s, b_raw.at[core_s])
    split_b(y_s, b_raw.at[y_s])
    wait(b_raw.at[far_s], b_sems, (2,), core_mate)
    split_b(far_s, b_raw.at[far_s])
    from_y(own_index, z)
    for n in range(n_trials):
        mix(n, z, x_own[n], first=True)
    mix_step(1)
    pass_all(n_cond - 1)
    pass_c(1)
    for step in range(2, n_cond):
        mix_step(step)

    @pl.loop(0, aux_dev)
    def _(p):
        for n in range(n_trials):
            high, low = split(mixed[n, p])
            m_high[n, p] = high
            m_low[n, p] = low

    apply(own_index, z)
    for step in range(1, n_cond):
        at_step(step, from_y)
        if step + 1 < n_cond:
            pass_c(step + 1)
        at_step(step, apply)
    finish(own_index, z)
    for step in range(1, n_cond):
        at_step(step, finish)

    def sent_out(index, block):
        copy(c_slot(y_s, block), c_slot(y_s, block), cf_sems, index, core_mate).wait_send()
        copy(y_part.at[block], y_got.at[block], y_sems, index, x_mate).wait_send()

    sent_out(own_index, z)
    for step in range(1, n_cond):
        at_step(step, sent_out)

    def under(where, run):
        if where is None:
            run()
        else:
            pl.when(where)(run)

    for src, dst, sems, index, mate, where in sent:
        under(where, lambda: copy(src, dst, sems, index, mate).wait_send())


def fused(n_state, n_cond, cond_pairs, val_pairs, screened, trials):
    aux_dev, rows, depth = cond_pairs.shape
    n_trials, _, width = trials.shape
    blk_v, blk_w = val_pairs.shape[1:]
    f32, bf16 = jnp.float32, jnp.bfloat16
    dma = pltpu.SemaphoreType.DMA
    vmem = pl.BlockSpec(memory_space=pltpu.VMEM)
    macs = aux_dev * n_trials * rows * width * (n_state * depth + width)
    return pl.pallas_call(
        functools.partial(kernel, n_cond),
        out_shape=jax.ShapeDtypeStruct(trials.shape, f32),
        in_specs=[pl.BlockSpec(memory_space=pltpu.SMEM), vmem, vmem, vmem],
        out_specs=vmem,
        scratch_shapes=[
            pltpu.VMEM(val_pairs.shape, f32),
            pltpu.VMEM((n_state, *cond_pairs.shape), f32),
            pltpu.VMEM((n_state, *cond_pairs.shape), bf16),
            pltpu.VMEM((n_state, *cond_pairs.shape), bf16),
            pltpu.VMEM((n_trials, n_cond, rows, width), f32),
            pltpu.VMEM((n_state, n_cond, *val_pairs.shape), f32),
            pltpu.VMEM((n_trials, aux_dev, rows, width), f32),
            pltpu.VMEM((n_trials, aux_dev, rows, width), bf16),
            pltpu.VMEM((n_trials, aux_dev, rows, width), bf16),
            pltpu.VMEM((n_cond, n_trials, rows, blk_w), f32),
            pltpu.VMEM((n_cond, n_trials, rows, blk_w), f32),
            dma((2, 1)),
            dma((2, 3)),
            dma((2, n_trials, 2, n_cond)),
            dma((2, n_trials, 2, n_cond)),
            dma((2, 2, n_cond)),
            dma((2, 2, n_cond)),
            dma((2, 2, n_cond)),
            dma((2, 2, n_cond)),
            dma((2, 2, n_cond)),
        ],
        compiler_params=pltpu.CompilerParams(
            collective_id=0, has_side_effects=True, vmem_limit_bytes=56 * 1024 * 1024
        ),
        cost_estimate=pl.CostEstimate(
            flops=6 * macs, bytes_accessed=4 * (2 * trials.size + cond_pairs.size), transcendentals=0
        ),
    )(screened, cond_pairs, val_pairs, trials)


def gathered(cond_pairs, val_pairs, screened, trials):
    aux_dev = cond_pairs.shape[0]
    aux_first = lax.axis_index("aux") * aux_dev
    own_rows = lax.dynamic_slice_in_dim(screened, aux_first, aux_dev, 0)
    coupled = jnp.einsum(
        "pq,qab->pab",
        own_rows,
        lax.all_gather(val_pairs, "aux", axis=0, tiled=True),
        precision=highest,
    )
    n_state = lax.axis_size("state")
    n_cond = lax.axis_size("cond")
    rows_state = coupled.shape[1]
    cols_cond = coupled.shape[2]
    pieces = lax.all_gather(coupled[None], ("state", "cond"), axis=0, tiled=True)
    coupled_full = pieces.reshape(n_state, n_cond, aux_dev, rows_state, cols_cond)
    coupled_full = coupled_full.transpose(2, 0, 3, 1, 4).reshape(
        aux_dev, n_state * rows_state, n_cond * cols_cond
    )
    everything = lax.all_gather(trials, "cond", axis=1, tiled=True)
    mixture = jnp.einsum(
        "pcd,ndv->pncv",
        lax.all_gather(cond_pairs, "state", axis=2, tiled=True),
        everything,
        precision=highest,
    )
    partial_value = jnp.einsum("pncv,pvw->ncw", mixture, coupled_full, precision=highest)
    return lax.psum(partial_value, "aux")


def solution(mesh):
    n_state, n_cond = mesh.shape["state"], mesh.shape["cond"]
    in_specs = (P("aux", "cond", "state"), P("aux", "state", "cond"), P(), P("state", "cond", None))
    out_specs = P("state", "cond", None)
    if mesh.shape["aux"] == 2 and n_state == 4 and n_cond == n_state:
        per_device = functools.partial(fused, n_state, n_cond)
    else:
        per_device = gathered
    return jax.shard_map(
        per_device, mesh=mesh, in_specs=in_specs, out_specs=out_specs, check_vma=False
    )
```

```python
import functools

import jax
import jax.numpy as jnp
from jax import lax
from jax.experimental import pallas as pl
from jax.experimental.pallas import tpu as pltpu
from jax.sharding import PartitionSpec as P

highest = lax.Precision.HIGHEST
MESH = pl.DeviceIdType.MESH
UP, DOWN = 0, 1


def split(value):
    high = value.astype(jnp.bfloat16)
    low = (value - high.astype(jnp.float32)).astype(jnp.bfloat16)
    return high, low


def dot3(a_high, a_low, b_high, b_low):
    dot = functools.partial(jnp.dot, preferred_element_type=jnp.float32)
    return dot(a_high, b_high) + dot(a_high, b_low) + dot(a_low, b_high)


def kernel(
    n_cond,
    screened,
    b_own,
    v_own,
    x_own,
    out,
    v_got,
    b_raw,
    b_high,
    b_low,
    x_raw,
    c_raw,
    mixed,
    m_high,
    m_low,
    y_part,
    y_got,
    v_sems,
    b_sems,
    xz_sems,
    xx_sems,
    cz_sems,
    cy_sems,
    ck_sems,
    cf_sems,
    y_sems,
    yo_sems,
):
    s = lax.axis_index("state")
    a = lax.axis_index("aux")
    z = lax.axis_index("cond")
    aux_dev, rows, depth = b_own.shape
    n_trials = x_own.shape[0]
    half = rows // 2
    blk_v, blk_w = v_own.shape[1], v_own.shape[2]
    core_s = s + 1 - 2 * lax.rem(s, 2)
    y_s = lax.rem(s + 2, 4)
    far_s = lax.rem(core_s + 2, 4)
    x_mate = {"aux": 1 - a}
    y_mate = {"state": y_s}
    core_mate = {"state": core_s}
    z_next = ({"cond": z + 1}, {"cond": z - 1})
    has_next = (z + 1 < n_cond, z > 0)

    barrier = pltpu.get_barrier_semaphore()
    for mate in (x_mate, y_mate, core_mate):
        pl.semaphore_signal(barrier, inc=1, device_id=mate, device_id_type=MESH)
    for way in (UP, DOWN):

        @pl.when(has_next[way])
        def _():
            pl.semaphore_signal(barrier, inc=1, device_id=z_next[way], device_id_type=MESH)

    pl.semaphore_wait(
        barrier, 3 + has_next[UP].astype(jnp.int32) + has_next[DOWN].astype(jnp.int32)
    )

    sent = []

    def copy(src, dst, sems, index, mate):
        return pltpu.make_async_remote_copy(
            src_ref=src,
            dst_ref=dst,
            send_sem=sems.at[(0, *index)],
            recv_sem=sems.at[(1, *index)],
            device_id=mate,
            device_id_type=MESH,
        )

    def send(src, dst, sems, index, mate, where=None):
        if where is None:
            copy(src, dst, sems, index, mate).start()
        else:

            @pl.when(where)
            def _():
                copy(src, dst, sems, index, mate).start()

        sent.append((src, dst, sems, index, mate, where))

    def wait(dst, sems, index, mate):
        copy(dst, dst, sems, index, mate).wait_recv()

    def arrives(way, step):
        return z - step >= 0 if way == UP else z + step < n_cond

    def origin(way, step):
        return z - step if way == UP else z + step

    def x_slot(n, block, side):
        return x_raw.at[n, block, pl.ds(side * half, half)]

    def send_x_own(n):
        for way in (UP, DOWN):
            send(
                x_own.at[n, pl.ds(a * half, half)],
                x_slot(n, z, a),
                xz_sems,
                (n, way, 1),
                z_next[way],
                has_next[way],
            )

    def pass_x(n, step):
        for way in (UP, DOWN):
            here = arrives(way, step)
            slot = x_slot(n, jnp.clip(origin(way, step), 0, n_cond - 1), a)

            @pl.when(here)
            def _():
                wait(slot, xz_sems, (n, way, step), z_next[way])

            if step + 1 < n_cond:
                send(
                    slot, slot, xz_sems, (n, way, step + 1), z_next[way],
                    jnp.logical_and(here, has_next[way]),
                )
            send(slot, slot, xx_sems, (n, way, step), x_mate, here)

    def c_slot(state, block):
        return c_raw.at[state, block]

    def pass_c(step):
        for way in (UP, DOWN):
            here = arrives(way, step)
            slot = c_slot(s, jnp.clip(origin(way, step), 0, n_cond - 1))

            @pl.when(here)
            def _():
                wait(slot, cz_sems, (way, step), z_next[way])

            if step + 1 < n_cond:
                send(
                    slot, slot, cz_sems, (way, step + 1), z_next[way],
                    jnp.logical_and(here, has_next[way]),
                )
            send(slot, slot, cy_sems, (way, step), y_mate, here)
            send(slot, slot, ck_sems, (way, step), core_mate, here)

    def split_b(state, source):
        for p in range(aux_dev):
            high, low = split(source[p])
            b_high[state, p] = high
            b_low[state, p] = low

    def mix(n, block, value, first=False):
        x_high, x_low = split(value)

        @pl.loop(0, aux_dev, unroll=2)
        def _(p):
            term = dot3(b_high[block, p], b_low[block, p], x_high, x_low)
            if first:
                mixed[n, p] = term
            else:
                mixed[n, p] += term

    def mix_step(n, step):
        for way in (UP, DOWN):
            here = arrives(way, step)
            block = jnp.clip(origin(way, step), 0, n_cond - 1)

            @pl.when(here)
            def _():
                wait(x_slot(n, block, 1 - a), xx_sems, (n, way, step), x_mate)
                mix(n, block, x_raw[n, block])

    def split_m(n):
        @pl.loop(0, aux_dev)
        def _(p):
            high, low = split(mixed[n, p])
            m_high[n, p] = high
            m_low[n, p] = low

    def from_y(index, block):
        slot = c_slot(y_s, block)
        wait(slot, cy_sems, index, y_mate)
        copy(slot, slot, cf_sems, index, core_mate).start()

    def respond(ns, block):
        @pl.loop(0, aux_dev, unroll=2)
        def _(p):
            c_high, c_low = split(c_raw[:, block, p].reshape(-1, blk_w))
            for n in ns:
                term = dot3(m_high[n, p], m_low[n, p], c_high, c_low)
                prior = y_part[block, n]
                y_part[block, n] = jnp.where(p == 0, term, prior + term)

    def wait_c(index, block):
        wait(c_slot(core_s, block), ck_sems, index, core_mate)
        wait(c_slot(far_s, block), cf_sems, index, core_mate)

    def apply(index, block):
        wait_c(index, block)
        respond(range(n_trials), block)
        copy(y_part.at[block], y_got.at[block], y_sems, index, x_mate).start()

    def apply_own(n):
        respond([n], z)
        send(y_part.at[z, n], y_got.at[z, n], yo_sems, (n,), x_mate)

    def finish(index, block):
        if index == own_index:
            for n in range(n_trials):
                wait(y_got.at[block, n], yo_sems, (n,), x_mate)
        else:
            wait(y_got.at[block], y_sems, index, x_mate)
        columns = pl.ds(pl.multiple_of(block * blk_w, blk_w), blk_w)
        for n in range(n_trials):
            out[n, :, columns] = y_part[block, n] + y_got[block, n]

    def at_step(step, *actions):
        for way in (UP, DOWN):
            block = jnp.clip(origin(way, step), 0, n_cond - 1)

            @pl.when(arrives(way, step))
            def _():
                for action in actions:
                    action((way, step), block)

    send(v_own, v_got, v_sems, (0,), x_mate)
    for n in range(n_trials):
        send_x_own(n)
    send(b_own, b_raw.at[s], b_sems, (0,), y_mate)
    send(b_own, b_raw.at[s], b_sems, (1,), core_mate)
    split_b(s, b_own)

    wait(v_got, v_sems, (0,), x_mate)
    for p in range(aux_dev):
        row = a * aux_dev + p
        total = screened[row, a * aux_dev] * v_own[0]
        for q in range(1, aux_dev):
            total += screened[row, a * aux_dev + q] * v_own[q]
        for q in range(aux_dev):
            total += screened[row, (1 - a) * aux_dev + q] * v_got[q]
        c_raw[s, z, p] = total
    own = c_slot(s, z)
    own_index = (UP, 0)
    send(own, own, cy_sems, own_index, y_mate)
    send(own, own, ck_sems, own_index, core_mate)

    def pass_all(step):
        for n in range(n_trials):
            pass_x(n, step)

    for step in range(1, n_cond - 1):
        pass_all(step)
    for way in (UP, DOWN):
        send(own, own, cz_sems, (way, 1), z_next[way], has_next[way])
    wait(b_raw.at[core_s], b_sems, (1,), core_mate)
    split_b(core_s, b_raw.at[core_s])
    wait(b_raw.at[y_s], b_sems, (0,), y_mate)
    send(b_raw.at[y_s], b_raw.at[y_s], b_sems, (2,), core_mate)
    split_b(y_s, b_raw.at[y_s])
    wait(b_raw.at[far_s], b_sems, (2,), core_mate)
    split_b(far_s, b_raw.at[far_s])
    from_y(own_index, z)
    for n in range(n_trials):
        mix(n, z, x_own[n], first=True)
        mix_step(n, 1)
    pass_all(n_cond - 1)
    pass_c(1)
    wait_c(own_index, z)
    for n in range(n_trials):
        for step in range(2, n_cond):
            mix_step(n, step)
        if n == n_trials - 1:
            at_step(1, from_y)
            pass_c(2)
        split_m(n)
        apply_own(n)

    for step in range(1, n_cond):
        if step > 1:
            at_step(step, from_y)
        if 1 < step < n_cond - 1:
            pass_c(step + 1)
        at_step(step, apply)
    finish(own_index, z)
    for step in range(1, n_cond):
        at_step(step, finish)

    def sent_out(index, block):
        copy(c_slot(y_s, block), c_slot(y_s, block), cf_sems, index, core_mate).wait_send()
        if index != own_index:
            copy(y_part.at[block], y_got.at[block], y_sems, index, x_mate).wait_send()

    sent_out(own_index, z)
    for step in range(1, n_cond):
        at_step(step, sent_out)

    def under(where, run):
        if where is None:
            run()
        else:
            pl.when(where)(run)

    for src, dst, sems, index, mate, where in sent:
        under(where, lambda: copy(src, dst, sems, index, mate).wait_send())


def fused(n_state, n_cond, cond_pairs, val_pairs, screened, trials):
    aux_dev, rows, depth = cond_pairs.shape
    n_trials, _, width = trials.shape
    blk_v, blk_w = val_pairs.shape[1:]
    f32, bf16 = jnp.float32, jnp.bfloat16
    dma = pltpu.SemaphoreType.DMA
    vmem = pl.BlockSpec(memory_space=pltpu.VMEM)
    macs = aux_dev * n_trials * rows * width * (n_state * depth + width)
    return pl.pallas_call(
        functools.partial(kernel, n_cond),
        out_shape=jax.ShapeDtypeStruct(trials.shape, f32),
        in_specs=[pl.BlockSpec(memory_space=pltpu.SMEM), vmem, vmem, vmem],
        out_specs=vmem,
        scratch_shapes=[
            pltpu.VMEM(val_pairs.shape, f32),
            pltpu.VMEM((n_state, *cond_pairs.shape), f32),
            pltpu.VMEM((n_state, *cond_pairs.shape), bf16),
            pltpu.VMEM((n_state, *cond_pairs.shape), bf16),
            pltpu.VMEM((n_trials, n_cond, rows, width), f32),
            pltpu.VMEM((n_state, n_cond, *val_pairs.shape), f32),
            pltpu.VMEM((n_trials, aux_dev, rows, width), f32),
            pltpu.VMEM((n_trials, aux_dev, rows, width), bf16),
            pltpu.VMEM((n_trials, aux_dev, rows, width), bf16),
            pltpu.VMEM((n_cond, n_trials, rows, blk_w), f32),
            pltpu.VMEM((n_cond, n_trials, rows, blk_w), f32),
            dma((2, 1)),
            dma((2, 3)),
            dma((2, n_trials, 2, n_cond)),
            dma((2, n_trials, 2, n_cond)),
            dma((2, 2, n_cond)),
            dma((2, 2, n_cond)),
            dma((2, 2, n_cond)),
            dma((2, 2, n_cond)),
            dma((2, 2, n_cond)),
            dma((2, n_trials)),
        ],
        compiler_params=pltpu.CompilerParams(
            collective_id=0, has_side_effects=True, vmem_limit_bytes=56 * 1024 * 1024
        ),
        cost_estimate=pl.CostEstimate(
            flops=6 * macs, bytes_accessed=4 * (2 * trials.size + cond_pairs.size), transcendentals=0
        ),
    )(screened, cond_pairs, val_pairs, trials)


def gathered(cond_pairs, val_pairs, screened, trials):
    aux_dev = cond_pairs.shape[0]
    aux_first = lax.axis_index("aux") * aux_dev
    own_rows = lax.dynamic_slice_in_dim(screened, aux_first, aux_dev, 0)
    coupled = jnp.einsum(
        "pq,qab->pab",
        own_rows,
        lax.all_gather(val_pairs, "aux", axis=0, tiled=True),
        precision=highest,
    )
    n_state = lax.axis_size("state")
    n_cond = lax.axis_size("cond")
    rows_state = coupled.shape[1]
    cols_cond = coupled.shape[2]
    pieces = lax.all_gather(coupled[None], ("state", "cond"), axis=0, tiled=True)
    coupled_full = pieces.reshape(n_state, n_cond, aux_dev, rows_state, cols_cond)
    coupled_full = coupled_full.transpose(2, 0, 3, 1, 4).reshape(
        aux_dev, n_state * rows_state, n_cond * cols_cond
    )
    everything = lax.all_gather(trials, "cond", axis=1, tiled=True)
    mixture = jnp.einsum(
        "pcd,ndv->pncv",
        lax.all_gather(cond_pairs, "state", axis=2, tiled=True),
        everything,
        precision=highest,
    )
    partial_value = jnp.einsum("pncv,pvw->ncw", mixture, coupled_full, precision=highest)
    return lax.psum(partial_value, "aux")


def solution(mesh):
    n_state, n_cond = mesh.shape["state"], mesh.shape["cond"]
    in_specs = (P("aux", "cond", "state"), P("aux", "state", "cond"), P(), P("state", "cond", None))
    out_specs = P("state", "cond", None)
    if mesh.shape["aux"] == 2 and n_state == 4 and n_cond == n_state:
        per_device = functools.partial(fused, n_state, n_cond)
    else:
        per_device = gathered
    return jax.shard_map(
        per_device, mesh=mesh, in_specs=in_specs, out_specs=out_specs, check_vma=False
    )
```
